128 devices in a mesh: sector: 16 (over x, z), span: 8 (over y, core).
Axes of the slice: x: 4, y: 4, z: 4, core: 2. Of those that a mesh axis runs over, the one named last changes fastest.
Arguments:
- state: float32 [216, 5, 8, 4096], P(None, None, 'span', 'sector'), may hold values from -6 to 6
- harmonics: float32 [17, 180, 8, 4096], P(None, None, 'span', 'sector'), may hold values from -3 to 3
- deriv: bfloat16 [3, 216, 216], replicated, may hold values from -0.4375 to 0.4375
- mixing: float32 [3, 5, 5], replicated, may hold values from -2.5 to 2.5
- metric: float32 [3, 8, 4096], P(None, 'span', 'sector'), may hold values from 0.5 to 2
- face_column: int32 [1536], P('sector'), may hold values from 0 to 255, as said below
- face_owner: int32 [1536], P('sector'), may hold values from 0 to 15, as said below
- partner: int32 [4096], P('sector'), may hold values from 0 to 255, as said below
- phase: int32 [4096], P('sector'), may hold values from 0 to 63
Outputs:
- new_state: float32 [216, 5, 8, 4096], P(None, None, 'span', 'sector')
The draws below stay inside these ranges and needn't reach their ends.
Inputs may be any that keep to these rules, and one draw needn't show every extreme that they name: `face_column`: the 96 columns of one sector block are distinct. `face_owner`: in the faces of one sector block no owner appears more than 16 times; one owner appears exactly 16 times in every sector block. `partner`: for each owner, a permutation of its 256 slots.
All inputs are finite; a program needn't handle non-finite values.
Results may differ from the reference program's by a relative error of at most 0.00043.
Values sent between devices are 32-bit elements; how exact they have to be, the bound alone decides.
A program may use at most 128 MiB of HBM per device.

```python
import math
import jax
import jax.numpy as jnp
from jax import lax

MODES = 216
FIELDS = 5
FACE_NODES = 36
HARMONICS = 8
PHASES = 64
COLS = 256
FACE_DEV = 96
SLOTS_OWN = 256
NBASIS = 17
LAYERS_ALL = 8
COLS_ALL = 4096
SLOTS_ALL = 4096
N_SECTOR = 16


def draw_face_column(key, part):
    key = jax.random.fold_in(key, 11)
    block_keys = jax.random.split(key, N_SECTOR)

    def one_block(block_key):
        return jax.random.permutation(block_key, COLS)[:FACE_DEV]
    return jax.vmap(one_block)(block_keys).reshape(-1).astype(jnp.int32)


def draw_face_owner(key, part):
    key = jax.random.fold_in(key, 23)
    busy_key, block_key = jax.random.split(key)
    busiest = jax.random.randint(busy_key, (), 0, N_SECTOR)
    capacity = SLOTS_OWN // N_SECTOR
    block_keys = jax.random.split(block_key, N_SECTOR)
    face_order = jnp.arange(FACE_DEV, dtype=jnp.int32)

    def one_block(block_key):
        turn_key, order_key = jax.random.split(block_key)
        turn = jax.random.randint(turn_key, (), 0, N_SECTOR - 1)
        others = (busiest + 1 + (face_order - capacity + turn) % (N_SECTOR - 1)) % N_SECTOR
        owners = jnp.where(face_order < capacity, busiest, others)
        return owners[jax.random.permutation(order_key, FACE_DEV)]
    return jax.vmap(one_block)(block_keys).reshape(-1).astype(jnp.int32)


def draw_partner(key, part):
    key = jax.random.fold_in(key, 37)
    owner_keys = jax.random.split(key, N_SECTOR)

    def one_owner(owner_key):
        return jax.random.permutation(owner_key, SLOTS_OWN)
    return jax.vmap(one_owner)(owner_keys).reshape(-1).astype(jnp.int32)


def with_ends(values, own_key, low, top_value):
    extent = values.shape
    spot = [jax.random.randint(jax.random.fold_in(own_key, axis), (), 0, extent[axis]) for axis in range(len(extent))]
    values = values.at[tuple(spot)].set(low)
    longest = extent.index(max(extent))
    spot[longest] = (spot[longest] + 1) % extent[longest]
    return values.at[tuple(spot)].set(top_value)


def block_scale(stream_key, shape, pieces, low, largest):
    gain = 1.0
    for dim, blocks in pieces:
        steps = jax.random.uniform(jax.random.fold_in(jax.random.fold_in(stream_key, 6), dim), (blocks,), jnp.float32, low / len(pieces), largest / len(pieces))
        gain = gain * jnp.repeat(jnp.exp(steps), shape[dim] // blocks).reshape((-1,) + (1,) * (len(shape) - 1 - dim))
    return gain


def bell_draw(own_key, extent, spread, bound, pieces=(), kind=jnp.bfloat16):
    array = spread * jax.random.normal(own_key, extent, jnp.float32)
    if pieces:
        array = array * block_scale(own_key, extent, pieces, -0.22, 0.18)
    return jnp.clip(array, -bound, bound).astype(kind)


def setup_inputs(seed: int = 0) -> dict:
    arg_keys = jax.random.split(jax.random.key(seed), 10)
    state = bell_draw(arg_keys[0], (MODES, FIELDS, LAYERS_ALL, COLS_ALL), 1.0, 6.0, ((2, 8), (3, 16)), jnp.float32)
    harmonics = bell_draw(arg_keys[1], (NBASIS, FACE_NODES * FIELDS, LAYERS_ALL, SLOTS_ALL), 0.3, 3.0, ((2, 8), (3, 16)), jnp.float32)
    deriv = bell_draw(arg_keys[2], (3, MODES, MODES), MODES ** -0.5, 0.4375)
    mixing = bell_draw(arg_keys[3], (3, FIELDS, FIELDS), FIELDS ** -0.5, 2.5, (), jnp.float32)
    metric = jnp.clip(jnp.exp(math.log(2.0) - 1.3862944 * jax.random.uniform(arg_keys[4], (3, LAYERS_ALL, COLS_ALL), jnp.float32) ** block_scale(arg_keys[4], (3, LAYERS_ALL, COLS_ALL), ((1, 8), (2, 16)), -0.2, 0.2)), 0.5, 2.0)
    face_column = draw_face_column(jax.random.fold_in(arg_keys[9], 71), 0)
    face_owner = draw_face_owner(jax.random.fold_in(arg_keys[9], 71), 0)
    partner = draw_partner(jax.random.fold_in(arg_keys[9], 71), 0)
    phase = with_ends(jax.random.randint(arg_keys[8], (SLOTS_ALL,), 0, PHASES), jax.random.fold_in(arg_keys[8], 1), 0, PHASES - 1).astype(jnp.int32)
    return {"state": state, "harmonics": harmonics, "deriv": deriv, "mixing": mixing, "metric": metric, "face_column": face_column, "face_owner": face_owner, "partner": partner, "phase": phase}


largest_value = lax.Precision.HIGHEST
step_size = 0.1
radial_penalty = 4.0
face_penalty = 4.0
relax_rate = 0.25
section_times = (0.0, 0.5, 0.5, 1.0)
section_weights = (1.0 / 6.0, 1.0 / 3.0, 1.0 / 3.0, 1.0 / 6.0)
section_advance = (0.5, 0.5, 1.0)


def basis_values(times):
    basis_rows = [jnp.ones_like(times)]
    for harmonic in range(1, HARMONICS + 1):
        phase_angle = (2.0 * math.pi * harmonic) * times
        basis_rows.append(jnp.cos(phase_angle))
        basis_rows.append(jnp.sin(phase_angle))
    return jnp.stack(basis_rows)


def projection(now_time):
    values = basis_values(jnp.asarray(now_time, jnp.float32))
    factor = jnp.where(jnp.arange(values.shape[0]) == 0, 1.0, 2.0).astype(jnp.float32)
    return values * factor


def owner_update(coefficients, received, slot_used, partner, phase, now_time):
    weights = projection(now_time)
    target_values = weights.reshape((-1,) + (1,) * received.ndim) * received[None]
    coefficients = coefficients + relax_rate * slot_used * (target_values - coefficients)
    shifted = basis_values(now_time + phase.astype(jnp.float32) / PHASES)
    ghosts = jnp.zeros(received.shape, jnp.float32)
    for basis_index in range(coefficients.shape[0]):
        ghosts = ghosts + jnp.take(coefficients[basis_index], partner, axis=-1) * shifted[basis_index]
    return coefficients, ghosts


def volume_term(section_state, deriv, mixing, metric):
    mode_count = section_state.shape[0]
    total = jnp.zeros(section_state.shape, jnp.float32)
    for direction in range(3):
        mixed = jnp.einsum('ij,mjlc->milc', mixing[direction], section_state, precision=largest_value)
        speed = jnp.tanh(section_state[:, 1 + direction])
        flux = (mixed + 0.5 * speed[:, None] * section_state).astype(jnp.bfloat16)
        slope = jnp.dot(deriv[direction], flux.reshape(mode_count, -1), preferred_element_type=jnp.float32)
        total = total - metric[direction][None, None] * slope.reshape(section_state.shape)
    return total


def radial_term(section_state):
    node_grid = section_state.reshape((6, FACE_NODES) + section_state.shape[1:])
    top_face = node_grid[5]
    bottom = node_grid[0]
    zero_rim = jnp.zeros_like(top_face[:, :, :1])
    upper_side = jnp.concatenate([bottom[:, :, 1:], zero_rim], axis=2)
    lower_side = jnp.concatenate([zero_rim, top_face[:, :, :-1]], axis=2)
    return radial_penalty * (upper_side - top_face), radial_penalty * (lower_side - bottom)


def assemble_rhs(volume, top_add, bottom_add, face_add):
    node_grid = volume.reshape((6, FACE_NODES) + volume.shape[1:])
    node_grid = node_grid.at[5].add(top_add).at[0].add(bottom_add)
    node_cube = node_grid.reshape((6, 6, 6) + volume.shape[1:])
    node_cube = node_cube.at[:, 0].add(face_add)
    return node_cube.reshape(volume.shape)


def build_routing(face_column, face_owner):
    capacity = SLOTS_OWN // N_SECTOR
    columns = face_column.reshape(N_SECTOR, FACE_DEV)
    owners = face_owner.reshape(N_SECTOR, FACE_DEV)
    face_order = jnp.arange(FACE_DEV, dtype=jnp.int32)
    earlier = face_order[None, :] < face_order[:, None]
    same_owner = owners[:, :, None] == owners[:, None, :]
    position = jnp.sum(same_owner & earlier[None], axis=2).astype(jnp.int32)
    destination = owners * capacity + position
    column_hot = (columns[:, :, None] == jnp.arange(COLS, dtype=jnp.int32)[None, None, :]).astype(jnp.float32)
    slot_hot = (destination[:, :, None] == jnp.arange(SLOTS_OWN, dtype=jnp.int32)[None, None, :]).astype(jnp.float32)
    return jnp.einsum('dkc,dks->dcs', column_hot, slot_hot, precision=largest_value)


def face_term(section_state, coefficients, routing_table, partner, phase, now_time):
    capacity = SLOTS_OWN // N_SECTOR
    layer_total = section_state.shape[2]
    face_rows = FACE_NODES * FIELDS
    node_cube = section_state.reshape(6, 6, 6, FIELDS, layer_total, N_SECTOR, COLS)
    trace_values = node_cube[:, 0].reshape(face_rows, layer_total, N_SECTOR, COLS)
    departing_traces = jnp.einsum('ziju,jup->zijp', trace_values, routing_table, precision=largest_value)
    departing_traces = departing_traces.reshape(face_rows, layer_total, N_SECTOR, N_SECTOR, capacity)
    received = jnp.transpose(departing_traces, (0, 1, 3, 2, 4)).reshape(face_rows, layer_total, SLOTS_ALL)
    slot_used = jnp.sum(routing_table, axis=1).reshape(N_SECTOR, N_SECTOR, capacity)
    slot_used = jnp.transpose(slot_used, (1, 0, 2)).reshape(SLOTS_ALL)
    owner_base = SLOTS_OWN * jnp.arange(N_SECTOR, dtype=jnp.int32)[:, None]
    partner_every_slot = (partner.reshape(N_SECTOR, SLOTS_OWN) + owner_base).reshape(SLOTS_ALL)
    coefficients, ghosts = owner_update(coefficients, received, slot_used, partner_every_slot, phase, now_time)
    returned_traces = ghosts.reshape(face_rows, layer_total, N_SECTOR, N_SECTOR, capacity)
    returned_traces = jnp.transpose(returned_traces, (0, 1, 3, 2, 4)).reshape(face_rows, layer_total, N_SECTOR, SLOTS_OWN)
    ghost_column_list = jnp.einsum('yigm,gtm->yigt', returned_traces, routing_table, precision=largest_value)
    has_face = jnp.sum(routing_table, axis=2)
    face_add = face_penalty * (ghost_column_list - trace_values * has_face)
    return face_add.reshape(6, 6, FIELDS, layer_total, COLS_ALL), coefficients


def reference(state, harmonics, deriv, mixing, metric, face_column, face_owner, partner, phase):
    routing_table = build_routing(face_column, face_owner)
    section_state = state
    coefficients = harmonics
    weighted_sum = jnp.zeros(state.shape, jnp.float32)
    for section_index in range(4):
        now_time = section_times[section_index] * step_size
        volume = volume_term(section_state, deriv, mixing, metric)
        top_add, bottom_add = radial_term(section_state)
        face_add, coefficients = face_term(section_state, coefficients, routing_table, partner, phase, now_time)
        rhs = assemble_rhs(volume, top_add, bottom_add, face_add)
        weighted_sum = weighted_sum + section_weights[section_index] * rhs
        if section_index < 3:
            section_state = state + (section_advance[section_index] * step_size) * rhs
    return state + step_size * weighted_sum
```

```python
import math

import jax
import jax.numpy as jnp
from jax import lax
from jax.experimental import pallas as pl
from jax.experimental.pallas import tpu as pltpu
from jax.sharding import PartitionSpec as P

MESH = pl.DeviceIdType.MESH
F32, BF16 = jnp.float32, jnp.bfloat16
FIELDS = 5
SIDE = 4
N = 16
SPAN = 8
FACES = 96
COLS = 256
ROWS = 240
EARLY, LATE = 192, 48
DT = 0.1
ADV = (0.05, 0.05, 0.1)
WGT = (1.0 / 6.0, 1.0 / 3.0, 1.0 / 3.0, 1.0 / 6.0)
STEP_OF = (0, 1, 1, 2)
KEEP = 0.75
RELAX = 0.25

FACE_TILES = ((32, 180), (40, 36), (48, 72), (56, 108), (64, 144), (72, 0))
REST_GROUPS = ((0, 186), (80, 6), (112, 42), (144, 78), (176, 114), (208, 150))


def nn(a, b):
    return lax.dot_general(a, b, (((1,), (0,)), ((), ())), preferred_element_type=F32)


def nt(a, b):
    return lax.dot_general(a, b, (((1,), (1,)), ((), ())), preferred_element_type=F32)


def tn(a, b):
    return lax.dot_general(a, b, (((0,), (0,)), ((), ())), preferred_element_type=F32)


def parts(a):
    high = a.astype(BF16)
    return high, (a - high.astype(F32)).astype(BF16)


def hot(condition):
    return condition.astype(F32).astype(BF16)


def iota(shape, dim):
    return lax.broadcasted_iota(jnp.int32, shape, dim)


def kernel(
    x_hbm, h_hbm, d_hbm, mix, met, fcol, fown, part, phase, o_hbm,
    xb, hb, db, xs, ys, vs, fe, fl, de, dl, coef, rt, pm, tb, gq, gp, ps, dcol, ub, pub, pr, gh,
    sf, rf, sg, rg, hup, hlo, cup, clo,
    lsem, fs, fr, gs, gr, hs, hr,
):
    me = lax.axis_index("sector")
    sp = lax.axis_index("span")
    mx, mz = me // SIDE, me % SIDE
    has_lower, has_upper = sp > 0, sp < SPAN - 1
    offsets = [(a, b) for a in range(SIDE) for b in range(SIDE) if (a, b) != (0, 0)]
    offsets.sort(key=lambda o: -(min(o[0], SIDE - o[0]) + min(o[1], SIDE - o[1])))

    def peer(o):
        return ((mx + o[0]) % SIDE) * SIDE + (mz + o[1]) % SIDE

    barrier = pltpu.get_barrier_semaphore()
    for o in offsets:
        pl.semaphore_signal(barrier, inc=1, device_id=(peer(o), sp), device_id_type=MESH)

    @pl.when(has_lower)
    def _():
        pl.semaphore_signal(barrier, inc=1, device_id=(me, sp - 1), device_id_type=MESH)

    @pl.when(has_upper)
    def _():
        pl.semaphore_signal(barrier, inc=1, device_id=(me, sp + 1), device_id_type=MESH)

    load_x = pltpu.make_async_copy(x_hbm, xb.at[pl.ds(0, 2160)], lsem.at[0])
    load_x.start()
    load_d = pltpu.make_async_copy(d_hbm, db, lsem.at[1])
    load_d.start()
    load_h = pltpu.make_async_copy(h_hbm, hb.at[pl.ds(0, 6120)], lsem.at[2])
    load_h.start()
    xb[pl.ds(2160, 32), :] = jnp.zeros((32, 128), F32)
    hb[pl.ds(6120, 40), :] = jnp.zeros((40, 128), F32)

    own = fown[...].reshape(1, FACES)
    own_hot = iota((N, FACES), 0) == own
    before = hot(iota((FACES, FACES), 0) < iota((FACES, FACES), 1))
    count = nn(hot(own_hot), before)
    position = jnp.sum(jnp.where(own_hot, count, 0.0), axis=0, keepdims=True)
    target = own * 16 + position.astype(jnp.int32)
    slot_hot = hot(iota((COLS, FACES), 0) == target)
    col_hot = hot(iota((COLS, FACES), 0) == fcol[...].reshape(1, FACES))
    route = nt(slot_hot, col_hot)
    rt[...] = route.astype(BF16)
    has_face = jnp.sum(route, axis=0, keepdims=True)
    eye = hot(iota((COLS, COLS), 0) == iota((COLS, COLS), 1))
    part_t = hot(iota((COLS, COLS), 0) == part[...].reshape(1, COLS))
    pm[...] = nt(eye, part_t).astype(BF16)
    row = iota((ROWS, COLS), 0)
    radial = jnp.where((row < 40) | ((row >= 72) & (row < 112)), 4.0, 0.0)
    coef[...] = radial + jnp.where((row >= 32) & (row < 80), 4.0 * has_face, 0.0)

    load_x.wait()
    for f in range(FIELDS):
        for h in range(2):
            for r0, m0 in FACE_TILES:
                xs[0, f, r0:r0 + 8, h * 128:h * 128 + 128] = xb[pl.ds((m0 * 5 + f) * 2 + h, 8, stride=10), :]


    tb[pl.ds(160, 16), :] = jnp.where(iota((16, COLS), 0) == 0, 1.0, 0.0)

    def fill_trace(section):
        def one(f, _):
            tb[pl.ds(pl.multiple_of(f * 32, 8), 32), :] = xs[section, f, 40:72, :]
            tb[pl.ds(pl.multiple_of(176 + f * 8, 8), 8), :] = xs[section, f, 72:80, :]
            tb[pl.ds(pl.multiple_of(216 + f * 8, 8), 8), :] = xs[section, f, 32:40, :]
            return _
        lax.fori_loop(0, FIELDS, one, 0)

    def send_all(src, dst, send_sem, recv_sem, e):
        for o in offsets:
            p = peer(o)
            pltpu.make_async_remote_copy(
                src_ref=src.at[e, p], dst_ref=dst.at[e, me], send_sem=send_sem.at[e], recv_sem=recv_sem.at[e],
                device_id=(p, sp), device_id_type=MESH,
            ).start()

    def wait_all(dst, sem, e):
        whole = dst.at[e, pl.ds(0, N - 1)]
        pltpu.make_async_copy(whole, whole, sem.at[e]).wait()

    def send_trace(e):
        high, low = parts(tb[...])
        picked = nt(rt[...], high) + nt(rt[...], low)
        sf[e] = picked.reshape(N, 16, COLS)
        if e == 0:
            arrivals = N - 1 + has_lower.astype(jnp.int32) + has_upper.astype(jnp.int32)
            pl.semaphore_wait(barrier, arrivals)
        send_all(sf, rf, fs, fr, e)
        rf[e, me] = sf[e, me]

    def halo(section, kind):
        up = kind < 2
        spans = ((0, 32), (32, 8), (80, 32), (72, 8))[kind]
        dst = (hlo, clo, hup, cup)[kind]
        return pltpu.make_async_remote_copy(
            src_ref=xs.at[section, :, pl.ds(spans[0], spans[1]), :], dst_ref=dst.at[section],
            send_sem=hs.at[section, kind], recv_sem=hr.at[section, kind],
            device_id=(me, sp + 1 if up else sp - 1), device_id_type=MESH,
        )

    def halo_send(section, corner):
        @pl.when(has_upper)
        def _():
            halo(section, corner).start()

        @pl.when(has_lower)
        def _():
            halo(section, 2 + corner).start()

    def halo_wait(section, corner):
        @pl.when(has_lower)
        def _():
            halo(section, corner).wait_recv()

        @pl.when(has_upper)
        def _():
            halo(section, 2 + corner).wait_recv()

    fill_trace(0)
    send_trace(0)
    halo_send(0, 1)
    for r0, m0 in REST_GROUPS:
        def one(f, _, r0=r0, m0=m0):
            for t in range(4):
                for h in range(2):
                    xs[0, f, r0 + 8 * t:r0 + 8 * t + 8, h * 128:h * 128 + 128] = (
                        xb[pl.ds((m0 + 8 * t) * 10 + f * 2 + h, 8, stride=10), :])
            return _
        lax.fori_loop(0, FIELDS, one, 0)
    halo_send(0, 0)

    @pl.when(jnp.logical_not(has_lower))
    def _():
        hlo[...] = jnp.zeros_like(hlo)
        clo[...] = jnp.zeros_like(clo)

    @pl.when(jnp.logical_not(has_upper))
    def _():
        hup[...] = jnp.zeros_like(hup)
        cup[...] = jnp.zeros_like(cup)

    load_d.wait()
    i = iota((ROWS, 216), 0)
    q8, q32 = i - 40, i - 112
    node = jnp.where(i < 40, jnp.where(i < 32, i + 186, i + 148), jnp.where(
        i < 72, 36 * ((q8 >> 3) + 1) + (q8 & 7), jnp.where(
            i < 80, i - 72, jnp.where(i < 112, i - 74, 36 * ((q32 >> 5) + 1) + 6 + (q32 & 31)))))
    in_face = (i >= 32) & (i < 80)
    local = jnp.where(in_face, i & 7, jnp.where(i < 32, i, jnp.where(i < 112, i - 80, q32 & 31)))
    valid = local < jnp.where(in_face, 6, 30)
    order = hot((node == iota((ROWS, 216), 1)) & valid)
    order_early = jnp.concatenate([order[0:32], order[80:ROWS]], axis=0)
    order_late = order[32:80]
    for k in range(3):
        moved = nn(order, db[k]).astype(BF16)
        de[k] = nt(moved, order_early).astype(BF16)
        dl[k] = nt(moved, order_late).astype(BF16)

    def flux_chunk(section, row0, dst, dst_row):
        v = [xs[section, f, pl.ds(row0, 16), :] for f in range(FIELDS)]
        for k in range(3):
            speed = 0.5 * jnp.tanh(v[1 + k])
            for f in range(FIELDS):
                total = speed * v[f]
                for j in range(FIELDS):
                    total = total + mix[f, k, j] * v[j]
                dst[k, f, pl.ds(dst_row, 16), :] = total.astype(BF16)

    def flux_early(section):
        def one(t, _):
            row0 = pl.multiple_of(16 * t + jnp.where(t >= 2, 48, 0), 16)
            flux_chunk(section, row0, fe, pl.multiple_of(16 * t, 16))
            return _
        lax.fori_loop(0, EARLY // 16, one, 0)

    def flux_late(section):
        def one(t, _):
            flux_chunk(section, pl.multiple_of(16 * t + 32, 16), fl, pl.multiple_of(16 * t, 16))
            return _
        lax.fori_loop(0, LATE // 16, one, 0)

    m = [met[k] for k in range(3)]

    def product_early():
        def one(f, _):
            total = m[0] * nn(de[0], fe[0, f])
            for k in (1, 2):
                total = total + m[k] * nn(de[k], fe[k, f])
            vs[f] = total
            return _
        lax.fori_loop(0, FIELDS, one, 0)

    def update(section, f, lo, hi):
        total = vs[f, lo:hi, :]
        for k in range(3):
            total = total + m[k] * nn(dl[k, lo:hi, :], fl[k, f])
        local = -total - coef[lo:hi, :] * xs[section, f, lo:hi, :]
        if section == 0:
            ys[f, lo:hi, :] = WGT[0] * local
        else:
            ys[f, lo:hi, :] += WGT[section] * local
        if section < 3:
            xs[section + 1, f, lo:hi, :] = xs[0, f, lo:hi, :] + ADV[section] * local

    def update_face(section):
        lax.fori_loop(0, FIELDS, lambda f, _: (update(section, f, 32, 80), _)[1], 0)

    def update_rest(section):
        def one(f, _):
            update(section, f, 0, 32)
            update(section, f, 80, ROWS)
            return _
        lax.fori_loop(0, FIELDS, one, 0)

    def add(section, f, lo, hi, value):
        ys[f, lo:hi, :] += (4.0 * WGT[section]) * value
        if section < 3:
            xs[section + 1, f, lo:hi, :] += (4.0 * ADV[section]) * value

    def add_corners(section):
        halo_wait(section, 1)

        def one(f, _):
            add(section, f, 32, 40, cup[section, f])
            add(section, f, 72, 80, clo[section, f])
            return _
        lax.fori_loop(0, FIELDS, one, 0)

    def add_rest(section):
        halo_wait(section, 0)

        def one(f, _):
            add(section, f, 0, 32, hup[section, f])
            add(section, f, 80, 112, hlo[section, f])
            return _
        lax.fori_loop(0, FIELDS, one, 0)

    def owner_tables():
        theta = phase[...].reshape(1, COLS).astype(F32) * (1.0 / 64.0)
        harmonic = (2.0 * math.pi) * (iota((8, COLS), 0) + 1).astype(F32)
        waves, kernels = [], []
        for s in range(3):
            angle = harmonic * (theta + 0.05 * s)
            cosine, sine = jnp.cos(angle), jnp.sin(angle)
            waves += [cosine, sine]
            kernels.append(1.0 + 2.0 * jnp.sum(cosine, axis=0, keepdims=True))
        high, low = parts(jnp.concatenate(waves, axis=0))
        ps[...] = nn(high, pm[...]) + nn(low, pm[...])
        high, low = parts(jnp.concatenate(kernels + [jnp.zeros((5, COLS), F32)], axis=0))
        columns = nt(eye, high) + nt(eye, low)
        for s in range(3):
            dcol[s] = jnp.broadcast_to(columns[:, s:s + 1], (COLS, 128))

    def ghost_start():
        load_h.wait()
        gq[:, pl.ds(160, 16), :] = jnp.zeros((3, 16, COLS), F32)

        def tile(t, _):
            f, r = t // 6, t % 6
            line = jnp.where(r == 0, 176 + 8 * f, jnp.where(r == 5, 216 + 8 * f, 32 * f + 8 * r - 8))
            line = pl.multiple_of(line, 8)
            for h in range(2):
                base = r * 60 + f * 2 + h
                lanes = slice(h * 128, h * 128 + 128)
                first = hb[pl.ds(base, 8, stride=10), :]
                sums = [first, first, first]
                for b in range(1, 17):
                    value = hb[pl.ds(base + b * 360, 8, stride=10), :]
                    w = (b - 1) // 2 + 8 * ((b - 1) % 2)
                    for s in range(3):
                        sums[s] = sums[s] + value * ps[16 * s + w:16 * s + w + 1, lanes]
                for s in range(3):
                    gq[s, pl.ds(line, 8), lanes] = sums[s]
            return _
        lax.fori_loop(0, 6 * FIELDS, tile, 0)
        for s in range(3):
            high, low = parts(gq[s])
            gp[s] = nt(pm[...], high) + nt(pm[...], low)

    def both(a):
        return jnp.concatenate([a, a], axis=1)

    def owner(section):
        wait_all(rf, fr, section)
        received = rf[section].reshape(COLS, COLS)
        if section > 0:
            received = received + (4.0 * ADV[section - 1]) * both(ub[...]) * gh[...]
        high, low = parts(received)
        moved = nn(pm[...], high) + nn(pm[...], low)
        if section == 0:
            ub[...] = jnp.broadcast_to(received[:, 160:161], (COLS, 128))
            pub[...] = jnp.broadcast_to(moved[:, 160:161], (COLS, 128))
        pr[section] = moved
        decay = 1.0 + (KEEP ** (section + 1) - 1.0) * pub[...]
        ghost = both(decay) * gp[STEP_OF[section]]
        for s in range(section + 1):
            lag = STEP_OF[section] - STEP_OF[s]
            ghost = ghost + both((RELAX * KEEP ** (section - s)) * dcol[lag]) * (moved if s == section else pr[s])
        gh[...] = ghost
        sg[section] = ghost.reshape(N, 16, COLS)
        send_all(sg, rg, gs, gr, section)
        rg[section, me] = sg[section, me]

    def add_ghost(section):
        wait_all(rg, gr, section)
        high, low = parts(rg[section].reshape(COLS, COLS))
        gq[0] = tn(high, rt[...]) + tn(low, rt[...])

        def one(f, _):
            add(section, f, 40, 72, gq[0, pl.ds(pl.multiple_of(f * 32, 8), 32), :])
            add(section, f, 72, 80, gq[0, pl.ds(pl.multiple_of(176 + f * 8, 8), 8), :])
            add(section, f, 32, 40, gq[0, pl.ds(pl.multiple_of(216 + f * 8, 8), 8), :])
            return _
        lax.fori_loop(0, FIELDS, one, 0)

    def face_part(section):
        flux_late(section)
        update_face(section)
        add_corners(section)
        if section < 3:
            fill_trace(section + 1)
            send_trace(section + 1)

    def rest_part(section):
        update_rest(section)
        add_rest(section)
        if section < 3:
            halo_send(section + 1, 0)
            flux_early(section + 1)
            product_early()

    def complete(section):
        add_ghost(section)
        halo_send(section + 1, 1)

    flux_early(0)
    product_early()
    face_part(0)
    owner_tables()
    ghost_start()
    owner(0)
    rest_part(0)
    owner(1)
    complete(0)
    face_part(1)
    rest_part(1)
    complete(1)
    face_part(2)
    owner(2)
    rest_part(2)
    owner(3)
    complete(2)
    face_part(3)
    rest_part(3)

    def store(f, lo, count, m0):
        for h in range(2):
            lanes = slice(h * 128, h * 128 + 128)
            value = xs[0, f, lo:lo + count, lanes] + DT * ys[f, lo:lo + count, lanes]
            xb[pl.ds(m0 * 10 + f * 2 + h, count, stride=10), :] = value

    for r0, m0 in REST_GROUPS:
        def one(f, _, r0=r0, m0=m0):
            for t in range(4):
                store(f, r0 + 8 * t, 8 if t < 3 else 6, m0 + 8 * t)
            return _
        lax.fori_loop(0, FIELDS, one, 0)
    add_ghost(3)

    def one(f, _):
        for r0, m0 in FACE_TILES:
            store(f, r0, 6, m0)
        return _
    lax.fori_loop(0, FIELDS, one, 0)
    result = pltpu.make_async_copy(xb.at[pl.ds(0, 2160)], o_hbm, lsem.at[3])
    result.start()

    for e in range(4):
        wait_all(sf, fs, e)
        wait_all(sg, gs, e)
        for corner in range(2):
            @pl.when(has_upper)
            def _(e=e, corner=corner):
                halo(e, corner).wait_send()

            @pl.when(has_lower)
            def _(e=e, corner=corner):
                halo(e, 2 + corner).wait_send()
    result.wait()


def shards(state, harmonics, deriv, mixing, metric, face_column, face_owner, partner, phase):
    any_ = pl.BlockSpec(memory_space=pl.ANY)
    vmem = pl.BlockSpec(memory_space=pltpu.VMEM)
    smem = pl.BlockSpec(memory_space=pltpu.SMEM)
    v = pltpu.VMEM
    dma = pltpu.SemaphoreType.DMA
    out = pl.pallas_call(
        kernel,
        out_shape=jax.ShapeDtypeStruct((2160, 128), F32),
        in_specs=[any_, any_, any_, smem, vmem, vmem, vmem, vmem, vmem],
        out_specs=any_,
        scratch_shapes=[
            v((2192, 128), F32), v((6160, 128), F32), v((3, 216, 216), BF16),
            v((4, FIELDS, ROWS, COLS), F32), v((FIELDS, ROWS, COLS), F32), v((FIELDS, ROWS, COLS), F32),
            v((3, FIELDS, EARLY, COLS), BF16), v((3, FIELDS, LATE, COLS), BF16),
            v((3, ROWS, EARLY), BF16), v((3, ROWS, LATE), BF16), v((ROWS, COLS), F32),
            v((COLS, COLS), BF16), v((COLS, COLS), BF16), v((COLS, COLS), F32),
            v((3, COLS, COLS), F32), v((3, COLS, COLS), F32), v((48, COLS), F32), v((3, COLS, 128), F32),
            v((COLS, 128), F32), v((COLS, 128), F32), v((4, COLS, COLS), F32), v((COLS, COLS), F32),
            v((4, N, 16, COLS), F32), v((4, N, 16, COLS), F32), v((4, N, 16, COLS), F32), v((4, N, 16, COLS), F32),
            v((4, FIELDS, 32, COLS), F32), v((4, FIELDS, 32, COLS), F32),
            v((4, FIELDS, 8, COLS), F32), v((4, FIELDS, 8, COLS), F32),
            dma((4,)), dma((4,)), dma((4,)), dma((4,)), dma((4,)), dma((4, 4)), dma((4, 4)),
        ],
        compiler_params=pltpu.CompilerParams(
            collective_id=0, has_side_effects=True, vmem_limit_bytes=56 << 20),
    )(state.reshape(2160, 128), harmonics.reshape(6120, 128), deriv, jnp.transpose(mixing, (1, 0, 2)), metric,
      face_column, face_owner, partner, phase)
    return out.reshape(state.shape)


def solution(mesh):
    field = P(None, None, "span", "sector")
    faces = P("sector")
    return jax.shard_map(
        shards,
        mesh=mesh,
        in_specs=(field, field, P(), P(), P(None, "span", "sector"), faces, faces, faces, faces),
        out_specs=field,
        check_vma=False,
    )
```
